32 devices in a mesh: row: 8 (over z, y), col: 4 (over x, core).
Axes of the slice: x: 2, y: 2, z: 4, core: 2. Of those that a mesh axis runs over, the one named last changes fastest.
Arguments:
- density: float32 [16, 4, 2, 128, 128], P('row', 'col'), as said below
- columns: int32 [16, 4, 2], P('row', 'col'), may hold values from -1 to 15, as said below
- owner_map: int32 [16], replicated, may hold values from 0 to 15, as said below
Outputs:
- purified: float32 [16, 4, 2, 128, 128], P('row', 'col')
The draws below stay inside these ranges and needn't reach their ends.
Inputs may be any that keep to these rules, and one draw needn't show every extreme that they name: `columns`: entry [s, c, e] names by its global number a block column of block row s whose slot lies in c * 4 to (c + 1) * 4 - 1, or is -1 (empty). No block column is named twice in a row. The pattern is symmetric: if row s names a column with slot t, row t names the column with slot s. Each block row names its own diagonal block and the block whose slot differs from s in the lowest bit. A permutation: owner_map[g] is the slot (the position along the first dimension of the arrays) of the block with global number g. `density`: the matrix is symmetric: the block of row s at column slot t is the transpose of the block of row t at column slot s. Blocks at empty entries are not part of the matrix.
All inputs are finite; a program needn't handle non-finite values.
Results may differ from the reference program's by a relative error of at most 0.000054.
Values sent between devices are 32-bit elements; how exact they have to be, the bound alone decides.
A program may use at most 128 MiB of HBM per device.

```python
import math
import jax
import jax.numpy as jnp
from jax import lax

B = 128
CAP = 2
NB = 16
BC = 4
KMAX = 8


def layout(key):
    groups = KMAX // CAP
    group_ids = jnp.arange(groups, dtype=jnp.int32)
    low_group = jnp.minimum(group_ids[:, None], group_ids[None, :])
    high_group = jnp.maximum(group_ids[:, None], group_ids[None, :])

    def pair_key(low_index, high_index):
        return jax.random.fold_in(jax.random.fold_in(key, low_index), high_index)
    pair_keys = jax.vmap(jax.vmap(pair_key))(low_group, high_group)

    def pair_perm(pair):
        return jax.random.permutation(pair, BC).astype(jnp.int32)

    def pair_first(pair):
        return jax.random.randint(jax.random.fold_in(pair, 1), (BC,), 0, 8)

    def pair_second(pair):
        return jax.random.randint(jax.random.fold_in(pair, 2), (BC,), 0, 16)
    permutes = jax.vmap(jax.vmap(pair_perm))(pair_keys)
    inverse = jnp.argsort(permutes, axis=-1, stable=True).astype(jnp.int32)
    level = jax.random.randint(jax.random.fold_in(key, 7001), (groups,), 1, 8)
    keep_first = jax.vmap(jax.vmap(pair_first))(pair_keys) < 7
    keep_second = jax.vmap(jax.vmap(pair_second))(pair_keys) < (level[low_group] + level[high_group])[..., None]
    row_slot = jnp.arange(NB, dtype=jnp.int32)
    own_group = (row_slot // BC)[:, None]
    position = (row_slot % BC)[:, None]
    other_group = group_ids[None, :]
    perm_rows = permutes[own_group, other_group]
    inverse_rows = inverse[own_group, other_group]
    first_rows = keep_first[own_group, other_group]
    second_rows = keep_second[own_group, other_group]
    spot = jnp.broadcast_to(position[:, :, None], (NB, groups, 1))

    def pick(table, where_at):
        return jnp.take_along_axis(table, where_at, axis=-1)[..., 0]
    upper_zero = pick(perm_rows, spot)
    upper_zero_ok = pick(first_rows, spot)
    upper_one = pick(perm_rows, (spot + 1) % BC)
    upper_one_ok = pick(second_rows, spot)
    back_zero = pick(inverse_rows, spot)
    lower_zero_ok = pick(first_rows, back_zero[..., None])
    back_one = (back_zero - 1) % BC
    lower_one_ok = pick(second_rows, back_one[..., None])
    upper = other_group > own_group
    lower = other_group < own_group
    own_pos = jnp.broadcast_to(position, (NB, groups))
    local_zero = jnp.where(upper, upper_zero, jnp.where(lower, back_zero, own_pos))
    ok_zero = jnp.where(upper, upper_zero_ok, jnp.where(lower, lower_zero_ok, True))
    local_one = jnp.where(upper, upper_one, jnp.where(lower, back_one, own_pos ^ 1))
    ok_one = jnp.where(upper, upper_one_ok, jnp.where(lower, lower_one_ok, True))
    slots = (other_group * BC)[..., None] + jnp.stack([local_zero, local_one], axis=-1)
    occupied = jnp.stack([ok_zero, ok_one], axis=-1)
    owner_map = jax.random.permutation(jax.random.fold_in(key, 7002), NB).astype(jnp.int32)
    global_of_slot = jnp.argsort(owner_map, stable=True).astype(jnp.int32)
    columns = jnp.where(occupied, global_of_slot[slots], -1).astype(jnp.int32)
    return (columns, owner_map, slots.astype(jnp.int32))


def draw_columns(key, part):
    return layout(key)[0]


def draw_owner_map(key, part):
    return layout(key)[1]


def draw_density(key, part):
    columns, owner_map, slots = layout(key)
    key = jax.random.fold_in(key, 11)
    row_slot = jnp.broadcast_to(jnp.arange(NB, dtype=jnp.int32)[:, None, None], slots.shape).reshape(-1)
    col_slot = slots.reshape(-1)
    low_slot = jnp.minimum(row_slot, col_slot)
    high_slot = jnp.maximum(row_slot, col_slot)

    def entry_key(low_index, high_index):
        return jax.random.fold_in(jax.random.fold_in(key, low_index), high_index)
    entry_keys = jax.vmap(entry_key)(low_slot, high_slot)

    def one_block(block_key):
        return jax.random.normal(block_key, (B, B), jnp.float32)
    raw = jax.vmap(one_block)(entry_keys)
    flipped = jnp.swapaxes(raw, -1, -2)
    same = (row_slot == col_slot)[:, None, None]
    below = (row_slot > col_slot)[:, None, None]
    value = jnp.where(same, (raw + flipped) * 0.70710678, jnp.where(below, flipped, raw))
    scale = 2.0 / math.sqrt(KMAX * B)
    return (value * scale).reshape(NB, KMAX // CAP, CAP, B, B).astype(jnp.float32)


def setup_inputs(seed: int = 0) -> dict:
    keys = jax.random.split(jax.random.key(seed), 4)
    return {
        "density": draw_density(jax.random.fold_in(keys[3], 71), 0),
        "columns": draw_columns(jax.random.fold_in(keys[3], 71), 0),
        "owner_map": draw_owner_map(jax.random.fold_in(keys[3], 71), 0),
    }


def reference(density, columns, owner_map):
    occupied = columns >= 0
    slot_of_entry = jnp.where(occupied, owner_map[jnp.clip(columns, 0, NB - 1)], 0).astype(jnp.int32)
    row_slot = jnp.broadcast_to(jnp.arange(NB, dtype=jnp.int32)[:, None, None], slot_of_entry.shape)
    masked = density * occupied[..., None, None].astype(density.dtype)
    tiled = jnp.zeros((NB, NB, B, B), jnp.float32).at[row_slot, slot_of_entry].add(masked)
    matrix = tiled.transpose(0, 2, 1, 3).reshape(NB * B, NB * B)
    square = jnp.dot(matrix, matrix, precision=lax.Precision.HIGHEST)
    cube = jnp.dot(square, matrix, precision=lax.Precision.HIGHEST)
    purified_full = 3.0 * square - 2.0 * cube
    purified_tiles = purified_full.reshape(NB, B, NB, B).transpose(0, 2, 1, 3)
    picked = purified_tiles[row_slot, slot_of_entry]
    return picked * occupied[..., None, None].astype(picked.dtype)
```

```python
import jax
import jax.numpy as jnp
from jax import lax
from jax.experimental import pallas as pl
from jax.experimental.pallas import tpu as pltpu
from jax.sharding import PartitionSpec as P

HIGHEST_PRECISION = lax.Precision.HIGHEST
MESH = pl.DeviceIdType.MESH
GROUPS = 4


def slot_of(block_ids, owner_map):
    block_total = owner_map.shape[0]
    matches = block_ids[..., None] == jnp.arange(block_total, dtype=jnp.int32)
    slots = jnp.sum(jnp.where(matches, owner_map, 0), axis=-1)
    return (slots, block_ids >= 0)


def column_entries(stored, stored_slots, stored_valid, queries, asked, first_slot):
    index = jnp.where(asked, queries, 0)
    blocks = stored[index]
    local_col = stored_slots[index] - first_slot
    present = stored_valid[index] & asked[:, None]
    return (blocks, local_col, present)


def shards(density, columns, owner_map):
    rows_here = density.shape[0]
    entry_cap = density.shape[2]
    block_size = density.shape[3]
    group_total = lax.axis_size("col")
    block_total = owner_map.shape[0]
    group_width = block_total // group_total
    column_index = lax.axis_index("col")
    first_slot = column_index * group_width
    row_vals, row_ids = (
        lax.all_gather(density, "col", axis=1, tiled=True),
        lax.all_gather(columns, "col", axis=1, tiled=True),
    )
    row_slots, row_valid = slot_of(row_ids, owner_map)
    col_vals, col_ids = (
        lax.all_gather(density, "row", axis=0, tiled=True),
        lax.all_gather(columns, "row", axis=0, tiled=True),
    )
    stored = col_vals[:, 0]
    stored_slots, stored_valid = slot_of(col_ids[:, 0], owner_map)

    def entries(queries, asked):
        return column_entries(stored, stored_slots, stored_valid, queries, asked, first_slot)

    local_ids = jnp.arange(group_width, dtype=jnp.int32)
    blocks, local_col, present = entries(row_slots.reshape(-1), row_valid.reshape(-1))
    left_blocks = row_vals.reshape(-1, block_size, block_size)
    products = jnp.einsum("qab,qfbc->qfac", left_blocks, blocks, precision=HIGHEST_PRECISION)
    weight = ((local_col[..., None] == local_ids) & present[..., None]).astype(jnp.float32)
    weight = weight.reshape(rows_here, -1, entry_cap, group_width)
    products = products.reshape(rows_here, -1, entry_cap, block_size, block_size)
    square = jnp.einsum("iqft,iqfac->itac", weight, products, precision=HIGHEST_PRECISION)
    found, found_col, found_ok = entries(row_slots.reshape(-1), row_valid.reshape(-1))
    pick_weight = ((found_col[..., None] == local_ids) & found_ok[..., None]).astype(jnp.float32)
    pick_weight = pick_weight.reshape(
        rows_here, 1 * lax.axis_size("col") * entry_cap, entry_cap, group_width
    )
    picked = jnp.einsum("iqft,itac->iqfac", pick_weight, square, precision=HIGHEST_PRECISION)
    found = found.reshape(
        rows_here, 1 * lax.axis_size("col") * entry_cap, entry_cap, block_size, block_size
    )
    partial_value = jnp.einsum("iqfac,iqfbc->iqab", picked, found, precision=HIGHEST_PRECISION)
    partial_value = partial_value.reshape(
        rows_here, 1 * lax.axis_size("col"), entry_cap, block_size, block_size
    )
    cubic = lax.psum_scatter(
        jnp.transpose(partial_value, (1, 0, 2, 3, 4)), "col", scatter_dimension=0, tiled=True
    )[0]
    own_slots, own_valid = slot_of(columns[:, 0], owner_map)
    own_pick = (((own_slots - first_slot)[..., None] == local_ids) & own_valid[..., None]).astype(
        jnp.float32
    )
    square_own = jnp.einsum("ift,itac->ifac", own_pick, square, precision=HIGHEST_PRECISION)
    purified = (3.0 * square_own - 2.0 * cubic) * own_valid[..., None, None].astype(jnp.float32)
    return purified[:, None]


def chosen(group, col):
    step = (col - group + GROUPS) % GROUPS
    middle = jnp.logical_or(group == 1, group == 2)
    return jnp.logical_or(step <= 1, jnp.logical_and(step == 2, middle))


def split(value):
    high = value.astype(jnp.bfloat16)
    low = (value - high.astype(jnp.float32)).astype(jnp.bfloat16)
    return high, low


def gather_kernel(
    den_ref, cols_ref, owner_ref, out_ref, units, mat_h, mat_l, sq_h, sq_l, sq_own, send_sem, recv_sem
):
    size = den_ref.shape[-1]
    row = lax.axis_index("row")
    col = lax.axis_index("col")
    z, y = row // 2, row % 2
    x, core = col // 2, col % 2

    def device(z_at, y_at, x_at, core_at):
        return {"row": z_at * 2 + y_at, "col": x_at * 2 + core_at}

    targets = {
        0: device(z + 1, y, x, core),
        1: device(z - 1, y, x, core),
        2: device(z, y, 1 - x, core),
        3: device(z, 1 - y, x, core),
        4: device(z, y, x, 1 - core),
    }
    there = {0: z < GROUPS - 1, 1: z > 0}

    barrier = pltpu.get_barrier_semaphore()
    for kind, target in targets.items():
        if kind in there:

            @pl.when(there[kind])
            def _():
                pl.semaphore_signal(barrier, inc=1, device_id=target, device_id_type=MESH)
        else:
            pl.semaphore_signal(barrier, inc=1, device_id=target, device_id_type=MESH)

    slots = []
    for i in range(2):
        pair = []
        for e in range(2):
            name = cols_ref[i, 0, e]
            place = owner_ref[jnp.maximum(name, 0)] - col * GROUPS
            pair.append(jnp.where(name >= 0, place, -1))
        slots.append(pair)
        own = units.at[row * 2 + i, col]
        for e in range(2):
            own[e * size : (e + 1) * size, :] = den_ref[i, 0, e]
        sub = lax.broadcasted_iota(jnp.int32, (8, size), 0)
        own[2 * size : 2 * size + 8, :] = jnp.where(sub == 0, pair[0], pair[1]).astype(jnp.float32)

    pl.semaphore_wait(barrier, 3 + there[0].astype(jnp.int32) + there[1].astype(jnp.int32))

    sends = []

    def copy(kind, s, c):
        return pltpu.make_async_remote_copy(
            src_ref=units.at[s, c],
            dst_ref=units.at[s, c],
            send_sem=send_sem.at[kind, s, c],
            recv_sem=recv_sem.at[s, c],
            device_id=targets[kind],
            device_id_type=MESH,
        )

    def start(kind, s, c, guard):
        pred = guard
        if kind in there:
            pred = jnp.logical_and(guard, there[kind])

        @pl.when(pred)
        def _():
            copy(kind, s, c).start()

        sends.append((pred, kind, s, c))

    def arrive(s, c, guard):
        @pl.when(guard)
        def _():
            copy(2, s, c).wait_recv()

    def planes(distance):
        if distance == 0:
            return [(z, jnp.bool_(True), None)]
        return [
            (z - distance, z - distance >= 0, 0),
            (z + distance, z + distance < GROUPS, 1),
        ]

    def lane(distance):
        for plane, inside, way in planes(distance):
            guard = jnp.logical_and(inside, chosen(plane, col))
            for h in range(2):
                s = plane * 4 + y * 2 + h
                if distance:
                    arrive(s, col, guard)
                for kind in (0, 1) if way is None else (way,):
                    start(kind, s, col, guard)
                for kind in (2, 3) if h == 0 else (3, 2):
                    start(kind, s, col, guard)
                start(4, s, col, guard)

    def near(distance):
        for plane, inside, _ in planes(distance):
            other = (1 - x) * 2 + core
            guard_x = jnp.logical_and(inside, chosen(plane, other))
            guard_y = jnp.logical_and(inside, chosen(plane, col))
            s = plane * 4 + y * 2
            t = plane * 4 + (1 - y) * 2
            arrive(s, other, guard_x)
            start(3, s, other, guard_x)
            start(4, s, other, guard_x)
            arrive(t + 1, col, guard_y)
            start(2, t + 1, col, guard_y)
            start(4, t + 1, col, guard_y)
            arrive(s + 1, other, guard_x)
            start(4, s + 1, other, guard_x)
            arrive(t, col, guard_y)
            start(4, t, col, guard_y)

    def corner(distance):
        for plane, inside, _ in planes(distance):
            other = (1 - x) * 2 + core
            guard = jnp.logical_and(inside, chosen(plane, other))
            for h in range(2):
                s = plane * 4 + (1 - y) * 2 + h
                arrive(s, other, guard)
                start(4, s, other, guard)

    def twin(distance):
        for plane, inside, _ in planes(distance):
            for x_at in range(2):
                other = x_at * 2 + 1 - core
                guard = jnp.logical_and(inside, chosen(plane, other))
                for i in range(4):
                    arrive(plane * 4 + i, other, guard)

    def dense(distance):
        for plane, inside, _ in planes(distance):
            for step in range(3):
                c = (plane + step) % GROUPS
                guard = inside
                if step == 2:
                    guard = jnp.logical_and(inside, chosen(plane, c))

                @pl.when(guard)
                def _():
                    @pl.loop(0, 4)
                    def _(i):
                        s = plane * 4 + i
                        unit = units.at[s, c]
                        places = [unit[2 * size + e : 2 * size + e + 1, :] for e in range(2)]
                        at_s = pl.ds(pl.multiple_of(s * size, size), size)
                        for way in range(1 if step == 0 else 2):
                            blocks = [unit[e * size : (e + 1) * size, :] for e in range(2)]
                            if way:
                                blocks = [b.T for b in blocks]
                            for j in range(4):
                                at_j = pl.ds(pl.multiple_of((c * 4 + j) * size, size), size)
                                value = jnp.where(
                                    places[0] == j,
                                    blocks[0],
                                    jnp.where(places[1] == j, blocks[1], 0.0),
                                )
                                high, low = split(value)
                                if way:
                                    mat_h[at_j, at_s] = high
                                    mat_l[at_j, at_s] = low
                                else:
                                    mat_h[at_s, at_j] = high
                                    mat_l[at_s, at_j] = low

    lane(0)
    lane(1)
    near(0)
    lane(2)
    near(1)
    corner(0)
    lane(3)
    near(2)
    corner(1)
    twin(0)
    dense(0)
    near(3)
    corner(2)
    twin(1)
    dense(1)
    corner(3)
    twin(2)
    dense(2)
    twin(3)
    dense(3)

    width = GROUPS * size

    def dot(a, b):
        return jnp.dot(a, b, preferred_element_type=jnp.float32)

    rows = pl.ds(pl.multiple_of(row * 2 * size, 2 * size), 2 * size)

    @pl.loop(0, GROUPS)
    def _(n):
        at = pl.ds(pl.multiple_of(n * width, width), width)
        a_h, a_l = mat_h[rows, :], mat_l[rows, :]
        part = dot(a_h, mat_h[:, at])
        part += dot(a_l, mat_h[:, at])
        part += dot(a_h, mat_l[:, at])
        high, low = split(part)
        sq_h[:, at] = high
        sq_l[:, at] = low

    at = pl.ds(pl.multiple_of(col * width, width), width)
    cube = dot(sq_h[...], mat_h[:, at])
    cube += dot(sq_l[...], mat_h[:, at])
    cube += dot(sq_h[...], mat_l[:, at])
    square = sq_h[:, at].astype(jnp.float32) + sq_l[:, at].astype(jnp.float32)
    sq_own[...] = 3.0 * square - 2.0 * cube
    for i in range(2):
        for e in range(2):
            value = jnp.zeros((size, size), jnp.float32)
            for j in range(4):
                block = sq_own[i * size : (i + 1) * size, j * size : (j + 1) * size]
                value = jnp.where(jnp.full((1, size), slots[i][e], jnp.int32) == j, block, value)
            out_ref[i, 0, e] = value

    for pred, kind, s, c in sends:

        @pl.when(pred)
        def _():
            copy(kind, s, c).wait_send()


def gathered(density, columns, owner_map):
    size = density.shape[3]
    total = owner_map.shape[0]
    width = GROUPS * size
    full = total * size
    return pl.pallas_call(
        gather_kernel,
        out_shape=jax.ShapeDtypeStruct(density.shape, jnp.float32),
        in_specs=[
            pl.BlockSpec(memory_space=pltpu.VMEM),
            pl.BlockSpec(memory_space=pltpu.SMEM),
            pl.BlockSpec(memory_space=pltpu.SMEM),
        ],
        out_specs=pl.BlockSpec(memory_space=pltpu.VMEM),
        scratch_shapes=[
            pltpu.VMEM((total, GROUPS, 2 * size + 8, size), jnp.float32),
            pltpu.VMEM((full, full), jnp.bfloat16),
            pltpu.VMEM((full, full), jnp.bfloat16),
            pltpu.VMEM((2 * size, full), jnp.bfloat16),
            pltpu.VMEM((2 * size, full), jnp.bfloat16),
            pltpu.VMEM((2 * size, width), jnp.float32),
            pltpu.SemaphoreType.DMA((5, total, GROUPS)),
            pltpu.SemaphoreType.DMA((total, GROUPS)),
        ],
        compiler_params=pltpu.CompilerParams(
            collective_id=0, has_side_effects=True, vmem_limit_bytes=48 * 2**20
        ),
    )(density, columns, owner_map)


def solution(mesh):
    in_specs = (P("row", "col", None, None, None), P("row", "col", None), P())
    out_specs = P("row", "col", None, None, None)
    small = mesh.shape["row"] == 2 * GROUPS and mesh.shape["col"] == GROUPS

    def program(density, columns, owner_map):
        fits = small and owner_map.shape[0] == 4 * GROUPS and density.shape[:3] == (2, 1, 2)
        if fits and density.shape[3] % 128 == 0 and density.shape[3] <= 128:
            return gathered(density, columns, owner_map)
        return shards(density, columns, owner_map)

    return jax.shard_map(program, mesh=mesh, in_specs=in_specs, out_specs=out_specs, check_vma=False)
```

```python
import functools

import jax
import jax.numpy as jnp
from jax import lax
from jax.experimental import pallas as pl
from jax.experimental.pallas import tpu as pltpu
from jax.sharding import PartitionSpec as P

HIGHEST_PRECISION = lax.Precision.HIGHEST
MESH = pl.DeviceIdType.MESH
GROUPS = 4


def slot_of(block_ids, owner_map):
    block_total = owner_map.shape[0]
    matches = block_ids[..., None] == jnp.arange(block_total, dtype=jnp.int32)
    slots = jnp.sum(jnp.where(matches, owner_map, 0), axis=-1)
    return (slots, block_ids >= 0)


def column_entries(stored, stored_slots, stored_valid, queries, asked, first_slot):
    index = jnp.where(asked, queries, 0)
    blocks = stored[index]
    local_col = stored_slots[index] - first_slot
    present = stored_valid[index] & asked[:, None]
    return (blocks, local_col, present)


def shards(density, columns, owner_map):
    rows_here = density.shape[0]
    entry_cap = density.shape[2]
    block_size = density.shape[3]
    group_total = lax.axis_size("col")
    block_total = owner_map.shape[0]
    group_width = block_total // group_total
    column_index = lax.axis_index("col")
    first_slot = column_index * group_width
    row_vals, row_ids = (
        lax.all_gather(density, "col", axis=1, tiled=True),
        lax.all_gather(columns, "col", axis=1, tiled=True),
    )
    row_slots, row_valid = slot_of(row_ids, owner_map)
    col_vals, col_ids = (
        lax.all_gather(density, "row", axis=0, tiled=True),
        lax.all_gather(columns, "row", axis=0, tiled=True),
    )
    stored = col_vals[:, 0]
    stored_slots, stored_valid = slot_of(col_ids[:, 0], owner_map)

    def entries(queries, asked):
        return column_entries(stored, stored_slots, stored_valid, queries, asked, first_slot)

    local_ids = jnp.arange(group_width, dtype=jnp.int32)
    blocks, local_col, present = entries(row_slots.reshape(-1), row_valid.reshape(-1))
    left_blocks = row_vals.reshape(-1, block_size, block_size)
    products = jnp.einsum("qab,qfbc->qfac", left_blocks, blocks, precision=HIGHEST_PRECISION)
    weight = ((local_col[..., None] == local_ids) & present[..., None]).astype(jnp.float32)
    weight = weight.reshape(rows_here, -1, entry_cap, group_width)
    products = products.reshape(rows_here, -1, entry_cap, block_size, block_size)
    square = jnp.einsum("iqft,iqfac->itac", weight, products, precision=HIGHEST_PRECISION)
    found, found_col, found_ok = entries(row_slots.reshape(-1), row_valid.reshape(-1))
    pick_weight = ((found_col[..., None] == local_ids) & found_ok[..., None]).astype(jnp.float32)
    pick_weight = pick_weight.reshape(
        rows_here, 1 * lax.axis_size("col") * entry_cap, entry_cap, group_width
    )
    picked = jnp.einsum("iqft,itac->iqfac", pick_weight, square, precision=HIGHEST_PRECISION)
    found = found.reshape(
        rows_here, 1 * lax.axis_size("col") * entry_cap, entry_cap, block_size, block_size
    )
    partial_value = jnp.einsum("iqfac,iqfbc->iqab", picked, found, precision=HIGHEST_PRECISION)
    partial_value = partial_value.reshape(
        rows_here, 1 * lax.axis_size("col"), entry_cap, block_size, block_size
    )
    cubic = lax.psum_scatter(
        jnp.transpose(partial_value, (1, 0, 2, 3, 4)), "col", scatter_dimension=0, tiled=True
    )[0]
    own_slots, own_valid = slot_of(columns[:, 0], owner_map)
    own_pick = (((own_slots - first_slot)[..., None] == local_ids) & own_valid[..., None]).astype(
        jnp.float32
    )
    square_own = jnp.einsum("ift,itac->ifac", own_pick, square, precision=HIGHEST_PRECISION)
    purified = (3.0 * square_own - 2.0 * cubic) * own_valid[..., None, None].astype(jnp.float32)
    return purified[:, None]


CHOSEN = (0, 2, 4, 5, 7, 9, 10, 11, 12, 15)


def chosen(group, col):
    place = group * GROUPS + col
    return functools.reduce(jnp.logical_or, [place == n for n in CHOSEN])


def split(value):
    high = value.astype(jnp.bfloat16)
    low = (value - high.astype(jnp.float32)).astype(jnp.bfloat16)
    return high, low


def gather_kernel(
    den_ref,
    cols_ref,
    owner_ref,
    out_ref,
    units,
    mat_h,
    mat_l,
    square,
    sq_h,
    sq_l,
    sq_own,
    given,
    taken,
    send_sem,
    recv_sem,
    local_sem,
    trade_sem,
):
    size = den_ref.shape[-1]
    row = lax.axis_index("row")
    col = lax.axis_index("col")
    z, y = row // 2, row % 2
    x, core = col // 2, col % 2

    def device(z_at, y_at, x_at, core_at):
        return {"row": z_at * 2 + y_at, "col": x_at * 2 + core_at}

    targets = {
        0: device(z + 1, y, x, core),
        1: device(z - 1, y, x, core),
        2: device(z, y, 1 - x, core),
        3: device(z, 1 - y, x, core),
        4: device(z, y, x, 1 - core),
    }
    there = {0: z < GROUPS - 1, 1: z > 0}

    barrier = pltpu.get_barrier_semaphore()
    for kind, target in targets.items():
        if kind in there:

            @pl.when(there[kind])
            def _():
                pl.semaphore_signal(barrier, inc=1, device_id=target, device_id_type=MESH)
        else:
            pl.semaphore_signal(barrier, inc=1, device_id=target, device_id_type=MESH)

    large = [
        pltpu.make_async_copy(
            den_ref.at[i, 0, e],
            units.at[row * 2 + i, col, pl.ds(e * size, size)],
            local_sem.at[i * 2 + e],
        )
        for i in range(2)
        for e in range(2)
    ]
    for item in large:
        item.start()
    slots = []
    sub = lax.broadcasted_iota(jnp.int32, (8, size), 0)
    for i in range(2):
        pair = []
        for e in range(2):
            name = cols_ref[i, 0, e]
            place = owner_ref[jnp.maximum(name, 0)] - col * GROUPS
            pair.append(jnp.where(name >= 0, place, -1))
        slots.append(pair)
        own = units.at[row * 2 + i, col]
        own[2 * size : 2 * size + 8, :] = jnp.where(sub == 0, pair[0], pair[1]).astype(jnp.float32)
    for item in large:
        item.wait()

    pl.semaphore_wait(barrier, 3 + there[0].astype(jnp.int32) + there[1].astype(jnp.int32))

    sends = []

    def copy(kind, s, c):
        return pltpu.make_async_remote_copy(
            src_ref=units.at[s, c],
            dst_ref=units.at[s, c],
            send_sem=send_sem.at[kind, s, c],
            recv_sem=recv_sem.at[s, c],
            device_id=targets[kind],
            device_id_type=MESH,
        )

    def start(kind, s, c, guard):
        pred = guard
        if kind in there:
            pred = jnp.logical_and(guard, there[kind])

        @pl.when(pred)
        def _():
            copy(kind, s, c).start()

        sends.append((pred, kind, s, c))

    def arrive(s, c, guard):
        @pl.when(guard)
        def _():
            copy(2, s, c).wait_recv()

    def planes(distance):
        if distance == 0:
            return [(z, jnp.bool_(True), None)]
        return [
            (z - distance, z - distance >= 0, 0),
            (z + distance, z + distance < GROUPS, 1),
        ]

    def lane(distance):
        for plane, inside, way in planes(distance):
            guard = jnp.logical_and(inside, chosen(plane, col))
            s = plane * 4 + y * 2
            ways = (0, 1) if way is None else (way,)
            for h in range(2):
                if distance:
                    arrive(s + h, col, guard)
                for kind in ways:
                    start(kind, s + h, col, guard)
                start(2 + h, s + h, col, guard)
            start(3, s, col, guard)
            start(2, s + 1, col, guard)
            for h in range(2):
                start(4, s + h, col, guard)

    def near(distance):
        for plane, inside, _ in planes(distance):
            other = (1 - x) * 2 + core
            guard_x = jnp.logical_and(inside, chosen(plane, other))
            guard_y = jnp.logical_and(inside, chosen(plane, col))
            s = plane * 4 + y * 2
            t = plane * 4 + (1 - y) * 2
            arrive(s, other, guard_x)
            start(3, s, other, guard_x)
            start(4, s, other, guard_x)
            arrive(t + 1, col, guard_y)
            start(2, t + 1, col, guard_y)
            start(4, t + 1, col, guard_y)
            arrive(s + 1, other, guard_x)
            start(4, s + 1, other, guard_x)
            arrive(t, col, guard_y)
            start(4, t, col, guard_y)

    def corner(distance):
        for plane, inside, _ in planes(distance):
            other = (1 - x) * 2 + core
            guard = jnp.logical_and(inside, chosen(plane, other))
            for h in range(2):
                s = plane * 4 + (1 - y) * 2 + h
                arrive(s, other, guard)
                start(4, s, other, guard)

    def twin(distance):
        for plane, inside, _ in planes(distance):
            for x_at in range(2):
                other = x_at * 2 + 1 - core
                guard = jnp.logical_and(inside, chosen(plane, other))
                for i in range(4):
                    arrive(plane * 4 + i, other, guard)

    def dense(distance):
        for plane, inside, _ in planes(distance):
            for step in range(4):
                c = (plane + step) % GROUPS
                guard = jnp.logical_and(inside, chosen(plane, c))

                @pl.when(guard)
                def _():
                    @pl.loop(0, 4)
                    def _(i):
                        s = plane * 4 + i
                        unit = units.at[s, c]
                        places = [unit[2 * size + e : 2 * size + e + 1, :] for e in range(2)]
                        at_s = pl.ds(pl.multiple_of(s * size, size), size)
                        for way in range(1 if step == 0 else 2):
                            blocks = [unit[e * size : (e + 1) * size, :] for e in range(2)]
                            if way:
                                blocks = [b.T for b in blocks]
                            for j in range(4):
                                at_j = pl.ds(pl.multiple_of((c * 4 + j) * size, size), size)
                                value = jnp.where(
                                    places[0] == j,
                                    blocks[0],
                                    jnp.where(places[1] == j, blocks[1], 0.0),
                                )
                                high, low = split(value)
                                if way:
                                    mat_h[at_j, at_s] = high
                                    mat_l[at_j, at_s] = low
                                else:
                                    mat_h[at_s, at_j] = high
                                    mat_l[at_s, at_j] = low

    width = GROUPS * size

    def dot(a, b):
        return jnp.dot(a, b, preferred_element_type=jnp.float32)

    rows = pl.ds(pl.multiple_of(row * 2 * size, 2 * size), 2 * size)

    def group_at(group):
        return pl.ds(pl.multiple_of(group * width, width), width)

    def away(a, b):
        gap = jnp.where(chosen(a, b), a, b) - z
        return jnp.maximum(gap, -gap)

    def squared(distance):
        @pl.loop(0, GROUPS * 2)
        def _(n):
            a, b = n // 2, (n % 2) * 2 + core

            @pl.when(jnp.maximum(away(z, a), away(a, b)) == distance)
            def _():
                at_a, at_b = group_at(a), group_at(b)
                a_h, a_l = mat_h[rows, at_a], mat_l[rows, at_a]
                part = dot(a_h, mat_h[at_a, at_b])
                part += dot(a_l, mat_h[at_a, at_b])
                part += dot(a_h, mat_l[at_a, at_b])
                square[:, at_b] += part

    def flush(keep):
        while len(sends) > keep:
            pred, kind, s, c = sends.pop(0)

            @pl.when(pred)
            def _():
                copy(kind, s, c).wait_send()

    def compute(distance):
        twin(distance)
        dense(distance)
        squared(distance)

    lane(0)
    square[...] = jnp.zeros_like(square)
    lane(1)
    near(0)
    lane(2)
    near(1)
    corner(0)
    twin(0)
    dense(0)
    lane(3)
    near(2)
    corner(1)
    squared(0)
    twin(1)
    dense(1)
    near(3)
    corner(2)
    squared(1)
    twin(2)
    dense(2)
    flush(60)
    corner(3)
    squared(2)
    flush(20)
    compute(3)

    @pl.loop(0, 2)
    def _(half):
        at = group_at(half * 2 + core)
        sq_h[:, at], sq_l[:, at] = split(square[:, at])

    def share(group):
        total = None
        for half in range(2):
            at_q, at = group_at(half * 2 + core), group_at(group)
            part = dot(sq_h[:, at_q], mat_h[at_q, at])
            part += dot(sq_l[:, at_q], mat_h[at_q, at])
            part += dot(sq_h[:, at_q], mat_l[at_q, at])
            total = part if total is None else total + part
        return total

    trade = pltpu.make_async_remote_copy(
        src_ref=given,
        dst_ref=taken,
        send_sem=trade_sem.at[0],
        recv_sem=trade_sem.at[1],
        device_id=targets[4],
        device_id_type=MESH,
    )
    given[...] = share(x * 2 + 1 - core)
    trade.start()
    sq_own[...] = 3.0 * square[:, group_at(col)] - 2.0 * share(col)
    flush(0)
    trade.wait()
    sq_own[...] -= 2.0 * taken[...]
    for i in range(2):
        for e in range(2):
            value = jnp.zeros((size, size), jnp.float32)
            for j in range(4):
                block = sq_own[i * size : (i + 1) * size, j * size : (j + 1) * size]
                value = jnp.where(jnp.full((1, size), slots[i][e], jnp.int32) == j, block, value)
            out_ref[i, 0, e] = value


def gathered(density, columns, owner_map):
    size = density.shape[3]
    total = owner_map.shape[0]
    width = GROUPS * size
    full = total * size
    return pl.pallas_call(
        gather_kernel,
        out_shape=jax.ShapeDtypeStruct(density.shape, jnp.float32),
        in_specs=[
            pl.BlockSpec(memory_space=pltpu.HBM),
            pl.BlockSpec(memory_space=pltpu.SMEM),
            pl.BlockSpec(memory_space=pltpu.SMEM),
        ],
        out_specs=pl.BlockSpec(memory_space=pltpu.VMEM),
        scratch_shapes=[
            pltpu.VMEM((total, GROUPS, 2 * size + 8, size), jnp.float32),
            pltpu.VMEM((full, full), jnp.bfloat16),
            pltpu.VMEM((full, full), jnp.bfloat16),
            pltpu.VMEM((2 * size, full), jnp.float32),
            pltpu.VMEM((2 * size, full), jnp.bfloat16),
            pltpu.VMEM((2 * size, full), jnp.bfloat16),
            pltpu.VMEM((2 * size, width), jnp.float32),
            pltpu.VMEM((2 * size, width), jnp.float32),
            pltpu.VMEM((2 * size, width), jnp.float32),
            pltpu.SemaphoreType.DMA((5, total, GROUPS)),
            pltpu.SemaphoreType.DMA((total, GROUPS)),
            pltpu.SemaphoreType.DMA((4,)),
            pltpu.SemaphoreType.DMA((2,)),
        ],
        compiler_params=pltpu.CompilerParams(
            collective_id=0, has_side_effects=True, vmem_limit_bytes=60 * 2**20
        ),
    )(density, columns, owner_map)


def solution(mesh):
    in_specs = (P("row", "col", None, None, None), P("row", "col", None), P())
    out_specs = P("row", "col", None, None, None)
    small = mesh.shape["row"] == 2 * GROUPS and mesh.shape["col"] == GROUPS

    def program(density, columns, owner_map):
        fits = small and owner_map.shape[0] == 4 * GROUPS and density.shape[:3] == (2, 1, 2)
        if fits and density.shape[3] % 128 == 0 and density.shape[3] <= 128:
            return gathered(density, columns, owner_map)
        return shards(density, columns, owner_map)

    return jax.shard_map(program, mesh=mesh, in_specs=in_specs, out_specs=out_specs, check_vma=False)
```
